32 devices in a mesh: head: 8 (over z, y), ctx: 4 (over x, core).
Axes of the slice: x: 2, y: 2, z: 4, core: 2. Of those that a mesh axis runs over, the one named last changes fastest.
Arguments:
- queries: bfloat16 [1024, 2048], P(('ctx', 'head')), may hold values from -9 to 9
- keys: bfloat16 [1024, 8192], P('ctx', 'head'), may hold values from -9 to 9
- values: bfloat16 [1024, 8192], P('ctx', 'head'), may hold values from -6 to 6
- routes: int32 [1024, 16], P(('ctx', 'head')), may hold values from 0 to 63, all different within a row; in each aligned block of 32 rows (0 to 31, 32 to 63, ...) at most 16 rows name the same one
- gates: float32 [1024, 16], P(('ctx', 'head')), may hold values from 0.25 to 1
- block_mask: int32 [8, 8], replicated, may hold values 0 or 1
- w_out: bfloat16 [8192, 8192], P('head'), may hold values from -0.125 to 0.125
Outputs:
- mixed: bfloat16 [1024, 8192], P(('ctx', 'head'))
The draws below stay inside these ranges and needn't reach their ends.
Inputs may be any that keep to these rules, and one draw needn't show every extreme that they name: `routes`: in each aligned block of 32 rows (the rows of one device) no head is named more than 16 times; each row names 16 different heads.
All inputs are finite; a program needn't handle non-finite values.
Results may differ from the reference program's by a relative error of at most 0.015.
Values may be sent and summed in bfloat16 or wider, within the bound.
A program may use at most 128 MiB of HBM per device.

```python
import math
import jax
import jax.numpy as jnp
import numpy as np
from jax import lax

D = 8192
H = 64
HD = 128
TOPH = 16
BLK = 128
TOK_DEV = 32
SEQ = 1024
CAP = 16
NB = 8
N_HEAD = 8


def draw_queries(key, part):
    fresh = jax.random.fold_in(key, 11)
    base = jnp.clip(jax.random.normal(fresh, (SEQ, TOPH, HD), jnp.float32), -6.0, 6.0)
    return base.reshape(SEQ, TOPH * HD).astype(jnp.bfloat16)


def draw_keys(key, part):
    fresh = jax.random.fold_in(key, 23)
    base = jnp.clip(jax.random.normal(fresh, (SEQ, H, HD), jnp.float32), -6.0, 6.0)
    return base.reshape(SEQ, H * HD).astype(jnp.bfloat16)


def set_ends(values, rng, low, top_value):
    shape = values.shape
    spot = [jax.random.randint(jax.random.fold_in(rng, axis), (), 0, shape[axis]) for axis in range(len(shape))]
    values = values.at[tuple(spot)].set(low)
    longest = shape.index(max(shape))
    spot[longest] = (spot[longest] + 1) % shape[longest]
    return values.at[tuple(spot)].set(top_value)


def block_levels(own_key, extent, split, smallest, high):
    def one(position, shards_of):
        steps = jax.random.uniform(jax.random.fold_in(jax.random.fold_in(own_key, 6), position), (shards_of,), jnp.float32, smallest / len(split), high / len(split))
        return jnp.repeat(jnp.exp(steps), extent[position] // shards_of).reshape((-1,) + (1,) * (len(extent) - position - 1))

    loudness = one(*split[0])
    for cut in split[1:]:
        loudness = loudness * one(*cut)
    return loudness


def deal_out(own_key, own, number, rows, count, top, reach, slope):
    order = jax.random.permutation(own_key, count)
    crowded, ordinary = portions_of(count, rows * top, reach, slope, True), portions_of(count, rows * top, reach, slope, False)
    places = jnp.arange(count)

    def named(sizes, offset_by):
        used = int((sizes > 0).sum())
        fixed = max(1, used // 4)
        passed = fixed + (places - fixed + offset_by * (used - fixed)) % max(1, count - fixed)
        return jnp.zeros((count,), jnp.int32).at[order[jnp.where(places < fixed, places, passed)]].set(jnp.asarray(sizes, jnp.int32))

    sizes = jnp.where(number % 4 == 0, named(crowded, number // 4), named(ordinary, number - number // 4 - 1))
    mixed = jax.random.permutation(jax.random.fold_in(own, 3), count)
    source_of, taker = mixed[0:count // 2 * 2:2], mixed[1:count // 2 * 2:2]
    margin = jnp.minimum(sizes[source_of] - 1, reach - sizes[taker]) // 2
    margin = jnp.where((source_of == order[0]) | (taker == order[0]) | (sizes[taker] == 0), 0, jnp.maximum(margin, 0))
    passed = jax.random.randint(jax.random.fold_in(own, 4), (count // 2,), 0, 1 << 20) % (margin + 1)
    sizes = sizes.at[source_of].add(-passed).at[taker].add(passed)
    members = jnp.searchsorted(jnp.cumsum(sizes), jnp.arange(rows * top), side="right").astype(jnp.int32)
    grid = members.reshape(top, rows).T
    grid = grid[jax.random.permutation(jax.random.fold_in(own, 1), rows)]
    offset_by = jax.random.randint(jax.random.fold_in(own, 2), (rows, 1), 0, top)
    return jnp.take_along_axis(grid, (jnp.arange(top)[None, :] + offset_by) % top, axis=1)


def portions_of(amount, total, bound, skew, full):
    weights = [(1 << 20) // math.isqrt(grade ** skew) + 1 for grade in range(1, amount + 1)]
    largest = bound if full else min(bound, max(-(-total // amount), total * weights[0] // sum(weights)))
    least = 1 if total - largest >= amount - 1 else 0
    given, rest = [largest] + [least] * (amount - 1), total - largest - least * (amount - 1)
    while rest > 0:
        free = [i for i in range(1, amount) if given[i] < largest] or [i for i in range(1, amount) if given[i] < bound]
        pool, remaining = sum([weights[i] for i in free]), rest
        for i in free:
            extra = min(bound - given[i], max(1, remaining * weights[i] // pool), rest)
            given[i] = given[i] + extra
            rest = rest - extra
    return np.array(given)


def noise(key, extent, deviation, most, split=(), kind=jnp.bfloat16):
    factor_of = block_levels(key, extent, split, -0.22, 0.18) if split else 1.0
    values = jax.random.normal(key, extent, jnp.float32) * deviation * factor_of
    return jnp.minimum(jnp.maximum(values, -most), most).astype(kind)


def setup_inputs(seed: int = 0) -> dict:
    arg_keys = jax.random.split(jax.random.key(seed), 8)
    queries = draw_queries(jax.random.fold_in(arg_keys[7], 71), 0)
    keys = draw_keys(jax.random.fold_in(arg_keys[7], 71), 0)
    values = noise(arg_keys[2], (SEQ, H * HD), 1.0, 6.0, ((0, 4), (1, 8)))
    routes_keys = jax.random.split(jax.random.fold_in(arg_keys[3], 1), SEQ // TOK_DEV)
    routes_turns = jax.random.permutation(jax.random.fold_in(arg_keys[3], 3), SEQ // TOK_DEV)
    routes = jax.vmap(lambda own, number: deal_out(jax.random.fold_in(arg_keys[3], 2), own, number, TOK_DEV, H, TOPH, CAP, 2))(routes_keys, routes_turns).reshape((SEQ, TOPH))
    gates = jnp.clip(jnp.exp(math.log(1.0) - 1.3862944 * jax.random.uniform(arg_keys[4], (SEQ, TOPH), jnp.float32) ** block_levels(arg_keys[4], (SEQ, TOPH), ((0, 32),), -0.2, 0.2)), 0.25, 1.0)
    block_mask = set_ends((jax.random.randint(arg_keys[5], (NB, NB), 0, 4) < 1).astype(jnp.int32), jax.random.fold_in(arg_keys[5], 1), 0, 1)
    w_out = noise(arg_keys[6], (H * HD, D), (TOPH * HD) ** -0.5, 0.125, ((0, 8),))
    return dict(queries=queries, keys=keys, values=values, routes=routes, gates=gates, block_mask=block_mask, w_out=w_out)


def reference(queries, keys, values, routes, gates, block_mask, w_out):
    seq_len = queries.shape[0]
    query_cube = queries.reshape(seq_len, TOPH, HD)
    key_cube = keys.reshape(seq_len, H, HD)
    value_cube = values.reshape(seq_len, H, HD)
    blocks = seq_len // BLK
    block_ids = jnp.arange(blocks, dtype=jnp.int32)
    usable = (block_ids[None, :] < block_ids[:, None]) & (block_mask == 1) | (block_ids[None, :] == block_ids[:, None])
    positions = jnp.arange(seq_len, dtype=jnp.int32)
    token_block = positions // BLK
    allowed = usable[token_block][:, token_block] & (positions[None, :] <= positions[:, None])
    score_scale = 1.0 / math.sqrt(HD)

    def one_head(head):
        chosen = routes == head
        own_query = lax.optimization_barrier(jnp.sum(jnp.where(chosen[:, :, None], query_cube.astype(jnp.float32), 0.0), axis=1)).astype(jnp.bfloat16)
        weight_sum = lax.optimization_barrier(jnp.sum(jnp.where(chosen, gates, 0.0), axis=1))
        head_keys = lax.dynamic_index_in_dim(key_cube, head, 1, keepdims=False)
        head_values = lax.dynamic_index_in_dim(value_cube, head, 1, keepdims=False)
        scores = jnp.dot(own_query, head_keys.T, preferred_element_type=jnp.float32) * score_scale
        scores = jnp.where(allowed, scores, -jnp.inf)
        peak = lax.optimization_barrier(jnp.max(scores, axis=1, keepdims=True))
        weights = jnp.exp(scores - peak)
        total = lax.optimization_barrier(jnp.sum(weights, axis=1, keepdims=True))
        mixed = jnp.dot(weights.astype(jnp.bfloat16), head_values, preferred_element_type=jnp.float32) / total
        return (mixed * weight_sum[:, None]).astype(jnp.bfloat16)
    heads_out = lax.map(one_head, jnp.arange(H, dtype=jnp.int32))
    weighted = heads_out.transpose(1, 0, 2).reshape(seq_len, H * HD)
    group = H // N_HEAD * HD

    def add_group(index, running):
        columns = lax.dynamic_slice_in_dim(weighted, index * group, group, 1)
        row_block = lax.dynamic_slice_in_dim(w_out, index * group, group, 0)
        term = jnp.dot(columns, row_block, preferred_element_type=jnp.float32)
        term = lax.optimization_barrier(term.astype(jnp.bfloat16)).astype(jnp.float32)
        return running + term
    summed = lax.fori_loop(0, N_HEAD, add_group, jnp.zeros((seq_len, D), jnp.float32))
    return summed.astype(jnp.bfloat16)
```

```python
import functools
import math

import jax
import jax.numpy as jnp
from jax import lax
from jax.experimental import pallas as pl
from jax.experimental.pallas import tpu as pltpu
from jax.sharding import PartitionSpec as P

HD = 128
BLK = 128
CHUNK = 512
MESH = pl.DeviceIdType.MESH


def kernel(
    n, ctxs,
    queries_ref, keys_ref, values_ref, routes_ref, gates_ref, mask_ref, w_hbm,
    out_ref,
    qf, rb, gb, qsend, gsend, qall, gall, kv, bias, weighted, w_ref,
    ysend, yrecv, psum, zrecv,
    w_sem, own_sem, x_send, x_recv, s_send, s_recv, q_send, q_recv, g_send, g_recv,
    y_send, y_recv, up_send, up_recv, dn_send, dn_recv,
):
    me = lax.axis_index("head")
    cx = lax.axis_index("ctx")
    y, z, m = lax.rem(me, 2), me // 2, n // 2
    core, chip, chips = lax.rem(cx, 2), cx // 2, ctxs // 2
    tok, topk = routes_ref.shape
    ctx_tok = keys_ref.shape[0]
    per_dev = keys_ref.shape[1] // HD
    rows = tok * n
    seq = ctx_tok * ctxs
    width = w_hbm.shape[1]
    cw = ysend.shape[2]
    count = width // cw
    parts = w_sem.shape[0]
    sources = (keys_ref, values_ref)

    def at(head, ctx):
        return (head, ctx)

    sibling = chip * 2 + (1 - core)

    barrier = pltpu.get_barrier_semaphore()
    for i in range(1, n):
        pl.semaphore_signal(barrier, inc=1, device_id=at(lax.rem(me + i, n), cx), device_id_type=MESH)
    pl.semaphore_signal(barrier, inc=1, device_id=at(me, sibling), device_id_type=MESH)

    @pl.when(chip > 0)
    def _():
        pl.semaphore_signal(barrier, inc=1, device_id=at(me, cx - 2), device_id_type=MESH)

    @pl.when(chip < chips - 1)
    def _():
        pl.semaphore_signal(barrier, inc=1, device_id=at(me, cx + 2), device_id_type=MESH)

    def own_rows(c):
        return pl.ds(pl.multiple_of(c * ctx_tok, ctx_tok), ctx_tok)

    def head_cols(h):
        return pl.ds(pl.multiple_of(h * HD, HD), HD)

    def own_copy(a, h):
        return pltpu.make_async_copy(
            sources[a].at[:, head_cols(h)], kv.at[a, h, own_rows(cx), :], own_sem.at[a, h]
        )

    @pl.loop(0, per_dev)
    def _(h):
        for a in range(2):
            own_copy(a, h).start()

    depth = w_hbm.shape[0] // parts

    def w_copy(i):
        return pltpu.make_async_copy(
            w_hbm.at[i * depth:(i + 1) * depth, :], w_ref.at[i * depth:(i + 1) * depth, :], w_sem.at[i]
        )

    for k in range(topk):
        qf[k] = queries_ref[:, k * HD:(k + 1) * HD].astype(jnp.float32)
        rb[k] = jnp.broadcast_to(routes_ref[:, k:k + 1], (tok, HD))
        gb[k] = jnp.broadcast_to(gates_ref[:, k:k + 1], (tok, HD))

    pl.semaphore_wait(
        barrier, n + (chip > 0).astype(jnp.int32) + (chip < chips - 1).astype(jnp.int32)
    )

    def x_copy(a, h, k):
        block = kv.at[a, h, own_rows(k * 2 + core), :]
        return pltpu.make_async_remote_copy(
            src_ref=block, dst_ref=block, send_sem=x_send.at[a, h, k], recv_sem=x_recv.at[a, h, k],
            device_id=at(me, cx + 2), device_id_type=MESH,
        )

    def x_first(a, h):
        return pltpu.make_async_remote_copy(
            src_ref=sources[a].at[:, head_cols(h)], dst_ref=kv.at[a, h, own_rows(cx), :],
            send_sem=x_send.at[a, h, chips - 1], recv_sem=x_recv.at[a, h, chip],
            device_id=at(me, cx + 2), device_id_type=MESH,
        )

    def s_copy(a, h, k):
        block = kv.at[a, h, own_rows(k * 2 + core), :]
        return pltpu.make_async_remote_copy(
            src_ref=block, dst_ref=block, send_sem=s_send.at[a, h, k], recv_sem=s_recv.at[a, h, k],
            device_id=at(me, sibling), device_id_type=MESH,
        )

    def s_wait(a, h, k):
        block = kv.at[a, h, own_rows(k * 2 + (1 - core)), :]
        pltpu.make_async_remote_copy(
            src_ref=block, dst_ref=block, send_sem=s_send.at[a, h, k], recv_sem=s_recv.at[a, h, k],
            device_id=at(me, sibling), device_id_type=MESH,
        ).wait_recv()

    @pl.when(chip < chips - 1)
    def _():
        @pl.loop(0, per_dev)
        def _(h):
            for a in range(2):
                x_first(a, h).start()

    def slot_of(source, dest):
        return lax.rem(source + dest, 2) * m + source // 2

    def q_copy(i):
        dest = lax.rem(me + i, n)
        return pltpu.make_async_remote_copy(
            src_ref=qsend.at[i], dst_ref=qall.at[slot_of(me, dest)], send_sem=q_send.at[i], recv_sem=q_recv.at[i],
            device_id=at(dest, cx), device_id_type=MESH,
        )

    def g_copy(i):
        dest = lax.rem(me + i, n)
        return pltpu.make_async_remote_copy(
            src_ref=gsend.at[i], dst_ref=gall.at[slot_of(me, dest)], send_sem=g_send.at[i], recv_sem=g_recv.at[i],
            device_id=at(dest, cx), device_id_type=MESH,
        )

    def spread(i):
        first = lax.rem(me + i, n) * per_dev
        acc = [jnp.zeros((tok, HD), jnp.float32) for _ in range(per_dev)]
        gate = jnp.zeros((tok, HD), jnp.float32)
        lane = lax.broadcasted_iota(jnp.int32, (tok, HD), 1) + first
        for k in range(topk):
            head, q = rb[k], qf[k]
            for j in range(per_dev):
                acc[j] = jnp.where(head == first + j, q, acc[j])
            gate = jnp.where(head == lane, gb[k], gate)
        return jnp.concatenate([a.astype(jnp.bfloat16) for a in acc], axis=1), gate

    @pl.loop(1, n)
    def _(i):
        q, gate = spread(i)
        qsend[i] = q
        gsend[i] = gate
        q_copy(i).start()
        g_copy(i).start()

    for i in range(parts):
        w_copy(i).start()

    q, gate = spread(0)
    qall[z] = q
    gall[z] = gate

    @pl.loop(0, per_dev)
    def _(h):
        for a in range(2):
            own_copy(a, h).wait()
            s_copy(a, h, chip).start()

    @pl.loop(0, n)
    def _(slot):
        source = lax.rem(slot, m) * 2 + jnp.where(slot < m, y, 1 - y)
        base = cx * ctx_tok + source * tok
        qblock = base // BLK
        row = mask_ref[pl.ds(qblock, 1), :]
        kpos = lax.broadcasted_iota(jnp.int32, (tok, seq), 1)
        qpos = lax.broadcasted_iota(jnp.int32, (tok, seq), 0) + base
        kstart = qblock * BLK
        usable = ((row > 0.5) & (kpos < kstart)) | (kpos >= kstart)
        bias[pl.ds(pl.multiple_of(slot * tok, tok), tok), :] = jnp.where(
            usable & (kpos <= qpos), 0.0, -1e30
        ).astype(bias.dtype)

    @pl.loop(chip * 2 + 2, ctxs)
    def _(c):
        @pl.loop(0, per_dev)
        def _(h):
            for a in range(2):
                kv[a, h, own_rows(c), :] = jnp.zeros((ctx_tok, HD), jnp.bfloat16)

    @pl.loop(1, n)
    def _(i):
        source = lax.rem(me + n - i, n)
        slot = slot_of(source, me)
        pltpu.make_async_remote_copy(
            src_ref=qsend.at[i], dst_ref=qall.at[slot], send_sem=q_send.at[i], recv_sem=q_recv.at[i],
            device_id=at(source, cx), device_id_type=MESH,
        ).wait_recv()
        pltpu.make_async_remote_copy(
            src_ref=gsend.at[i], dst_ref=gall.at[slot], send_sem=g_send.at[i], recv_sem=g_recv.at[i],
            device_id=at(source, cx), device_id_type=MESH,
        ).wait_recv()

    scale = math.log2(math.e) / math.sqrt(HD)
    tile = max(tok, min(rows, (256 * 1024 // seq) // tok * tok))

    def forward(h):
        @pl.loop(0, chip)
        def _(k):
            for a in range(2):
                x_copy(a, h, k).wait_recv()
                s_copy(a, h, k).start()

            @pl.when(chip < chips - 1)
            def _():
                for a in range(2):
                    x_copy(a, h, k).start()

    def attend(h):
        @pl.loop(0, chip + 1)
        def _(k):
            for a in range(2):
                s_wait(a, h, k)

        def one(t):
            group = pl.ds(t * (tile // tok), tile // tok)
            here = pl.ds(pl.multiple_of(t * tile, tile), tile)
            q = qall[group, :, head_cols(h)].reshape(tile, HD)
            s = lax.dot_general(q, kv[0, h], (((1,), (1,)), ((), ())), preferred_element_type=jnp.float32)
            s = s * scale + bias[here, :].astype(jnp.float32)
            p = jnp.exp2(s - jnp.max(s, axis=1, keepdims=True))
            total = jnp.sum(p, axis=1, keepdims=True)
            o = jnp.dot(p.astype(jnp.bfloat16), kv[1, h], preferred_element_type=jnp.float32)
            lane = lax.broadcasted_iota(jnp.int32, (tile, HD), 1)
            gates = gall[group].reshape(tile, HD)
            g = jnp.sum(jnp.where(lane == h, gates, 0.0), axis=1, keepdims=True)
            weighted[here, head_cols(h)] = (o * (g / total)).astype(jnp.bfloat16)

        if rows == tile:
            one(0)
        else:
            pl.loop(0, rows // tile)(one)

    @pl.loop(0, per_dev + 1)
    def _(h):
        @pl.when(h < per_dev)
        def _():
            forward(h)

        @pl.when(h >= 1)
        def _():
            attend(h - 1)

    for i in range(parts):
        w_copy(i).wait()

    half = m * tok

    def y_copy(c):
        return pltpu.make_async_remote_copy(
            src_ref=ysend.at[c], dst_ref=yrecv.at[c], send_sem=y_send.at[c], recv_sem=y_recv.at[c],
            device_id=at(z * 2 + 1 - y, cx), device_id_type=MESH,
        )

    def up_copy(c, d):
        return pltpu.make_async_remote_copy(
            src_ref=psum.at[c, d], dst_ref=zrecv.at[c, d + 1], send_sem=up_send.at[c, d], recv_sem=up_recv.at[c, d],
            device_id=at(me + 2, cx), device_id_type=MESH,
        )

    def dn_copy(c, d):
        return pltpu.make_async_remote_copy(
            src_ref=psum.at[c, d], dst_ref=zrecv.at[c, d], send_sem=dn_send.at[c, d], recv_sem=dn_recv.at[c, d],
            device_id=at(me - 2, cx), device_id_type=MESH,
        )

    def add(c, d, got):
        psum[c, d] = (psum[c, d].astype(jnp.float32) + zrecv[c, got].astype(jnp.float32)).astype(jnp.bfloat16)

    @pl.loop(0, count + m)
    def _(i):
        @pl.when(i < count)
        def _():
            part = jnp.dot(
                weighted[...], w_ref[:, pl.ds(pl.multiple_of(i * cw, cw), cw)],
                preferred_element_type=jnp.float32,
            ).astype(jnp.bfloat16)
            ysend[i] = part[half:]
            psum[i] = part[:half].reshape(m, tok, cw)
            y_copy(i).start()

        @pl.when((i >= 1) & (i <= count))
        def _():
            c = i - 1
            y_copy(c).wait_recv()
            psum[c] = (
                psum[c].astype(jnp.float32) + yrecv[c].astype(jnp.float32).reshape(m, tok, cw)
            ).astype(jnp.bfloat16)

        cu = i - 1 - z
        cd = i - 1 - (m - 1 - z)

        @pl.when((cu >= 0) & (cu < count))
        def _():
            for d in range(m - 1, -1, -1):
                @pl.when((z > 0) & (z <= d))
                def _():
                    up_copy(cu, d).wait_recv()

                @pl.when(z < d)
                def _():
                    @pl.when(z > 0)
                    def _():
                        add(cu, d, d + 1)
                    up_copy(cu, d).start()

        @pl.when((cd >= 0) & (cd < count))
        def _():
            for d in range(m):
                @pl.when((z < m - 1) & (z >= d))
                def _():
                    dn_copy(cd, d).wait_recv()

                @pl.when(z > d)
                def _():
                    @pl.when(z < m - 1)
                    def _():
                        add(cd, d, d)
                    dn_copy(cd, d).start()

        @pl.when(i >= m)
        def _():
            c = i - m
            cols = pl.ds(pl.multiple_of(c * cw, cw), cw)
            for d in range(m):
                @pl.when(z == d)
                def _():
                    total = psum[c, d].astype(jnp.float32)
                    if d > 0:
                        total = total + zrecv[c, d + 1].astype(jnp.float32)
                    if d < m - 1:
                        total = total + zrecv[c, d].astype(jnp.float32)
                    out_ref[:, cols] = total.astype(jnp.bfloat16)

    @pl.loop(0, count)
    def _(c):
        y_copy(c).wait_send()
        for d in range(m):
            @pl.when(z < d)
            def _():
                up_copy(c, d).wait_send()

            @pl.when(z > d)
            def _():
                dn_copy(c, d).wait_send()

    @pl.loop(1, n)
    def _(i):
        q_copy(i).wait_send()
        g_copy(i).wait_send()

    @pl.loop(0, per_dev)
    def _(h):
        for a in range(2):
            @pl.loop(0, chip + 1)
            def _(k):
                s_copy(a, h, k).wait_send()

            @pl.when(chip < chips - 1)
            def _():
                x_first(a, h).wait_send()

                @pl.loop(0, chip)
                def _(k):
                    x_copy(a, h, k).wait_send()


def local(n, ctxs, queries, keys, values, routes, gates, block_mask, w_out):
    tok, topk = routes.shape
    ctx_tok, held = keys.shape
    per_dev = held // HD
    seq = ctx_tok * ctxs
    rows = tok * n
    depth, width = w_out.shape
    m = n // 2
    chips = ctxs // 2
    blocks = block_mask.shape[0]
    mask = jnp.broadcast_to(block_mask.astype(jnp.float32)[:, :, None], (blocks, blocks, BLK)).reshape(blocks, seq)
    count = width // CHUNK
    bf, f32, dma = jnp.bfloat16, jnp.float32, pltpu.SemaphoreType.DMA
    vmem = pl.BlockSpec(memory_space=pltpu.VMEM)
    hbm = pl.BlockSpec(memory_space=pl.ANY)
    return pl.pallas_call(
        functools.partial(kernel, n, ctxs),
        out_shape=jax.ShapeDtypeStruct((tok, width), bf),
        in_specs=[vmem, hbm, hbm, vmem, vmem, vmem, hbm],
        out_specs=vmem,
        scratch_shapes=[
            pltpu.VMEM((topk, tok, HD), f32),
            pltpu.VMEM((topk, tok, HD), jnp.int32),
            pltpu.VMEM((topk, tok, HD), f32),
            pltpu.VMEM((n, tok, held), bf),
            pltpu.VMEM((n, tok, HD), f32),
            pltpu.VMEM((n, tok, held), bf),
            pltpu.VMEM((n, tok, HD), f32),
            pltpu.VMEM((2, per_dev, seq, HD), bf),
            pltpu.VMEM((rows, seq), bf),
            pltpu.VMEM((rows, held), bf),
            pltpu.VMEM((depth, width), bf),
            pltpu.VMEM((count, m * tok, CHUNK), bf),
            pltpu.VMEM((count, m * tok, CHUNK), bf),
            pltpu.VMEM((count, m, tok, CHUNK), bf),
            pltpu.VMEM((count, m + 1, tok, CHUNK), bf),
            dma((8,)),
            dma((2, per_dev)),
            dma((2, per_dev, chips)),
            dma((2, per_dev, chips)),
            dma((2, per_dev, chips)),
            dma((2, per_dev, chips)),
            dma((n,)),
            dma((n,)),
            dma((n,)),
            dma((n,)),
            dma((count,)),
            dma((count,)),
            dma((count, m)),
            dma((count, m)),
            dma((count, m)),
            dma((count, m)),
        ],
        compiler_params=pltpu.CompilerParams(
            collective_id=0, has_side_effects=True, vmem_limit_bytes=63 * 1024 * 1024
        ),
    )(queries, keys, values, routes, gates, mask, w_out)


def solution(mesh):
    placed = (
        P(("ctx", "head"), None),
        P("ctx", "head"),
        P("ctx", "head"),
        P(("ctx", "head"), None),
        P(("ctx", "head"), None),
        P(),
        P("head", None),
    )
    return jax.shard_map(
        functools.partial(local, mesh.shape["head"], mesh.shape["ctx"]),
        mesh=mesh, in_specs=placed, out_specs=P(("ctx", "head"), None), check_vma=False,
    )
```

```python
import functools
import math

import jax
import jax.numpy as jnp
from jax import lax
from jax.experimental import pallas as pl
from jax.experimental.pallas import tpu as pltpu
from jax.sharding import PartitionSpec as P

HD = 128
BLK = 128
CHUNK = 512
LAG = 4
MESH = pl.DeviceIdType.MESH


def kernel(
    n, ctxs,
    queries_ref, keys_ref, values_ref, routes_ref, gates_ref, mask_ref, w_hbm,
    out_ref,
    mask_scr, qf, rb, gb, qsend, gsend, qall, gall, kv, bias, weighted, w_ref,
    ysend, yrecv, psum, zrecv,
    w_sem, own_sem, x_send, x_recv, s_send, s_recv, q_send, q_recv, g_send, g_recv,
    y_send, y_recv, up_send, up_recv, dn_send, dn_recv,
):
    me = lax.axis_index("head")
    cx = lax.axis_index("ctx")
    y, z, m = lax.rem(me, 2), me // 2, n // 2
    core, chip, chips = lax.rem(cx, 2), cx // 2, ctxs // 2
    topk, tok = routes_ref.shape
    ctx_tok = keys_ref.shape[0]
    per_dev = keys_ref.shape[1] // HD
    rows = tok * n
    seq = ctx_tok * ctxs
    width = w_hbm.shape[1]
    cw = ysend.shape[2]
    count = width // cw
    parts = w_sem.shape[0]
    sources = (keys_ref, values_ref)

    def at(head, ctx):
        return (head, ctx)

    sibling = chip * 2 + (1 - core)

    barrier = pltpu.get_barrier_semaphore()
    for i in range(1, n):
        pl.semaphore_signal(barrier, inc=1, device_id=at(lax.rem(me + i, n), cx), device_id_type=MESH)
    pl.semaphore_signal(barrier, inc=1, device_id=at(me, sibling), device_id_type=MESH)

    @pl.when(chip > 0)
    def _():
        pl.semaphore_signal(barrier, inc=1, device_id=at(me, cx - 2), device_id_type=MESH)

    @pl.when(chip < chips - 1)
    def _():
        pl.semaphore_signal(barrier, inc=1, device_id=at(me, cx + 2), device_id_type=MESH)

    def own_rows(c):
        return pl.ds(pl.multiple_of(c * ctx_tok, ctx_tok), ctx_tok)

    def head_cols(h):
        return pl.ds(pl.multiple_of(h * HD, HD), HD)

    def own_copy(a, h):
        return pltpu.make_async_copy(
            sources[a].at[:, head_cols(h)], kv.at[a, h, own_rows(cx), :], own_sem.at[a, h]
        )

    @pl.loop(0, per_dev)
    def _(h):
        for a in range(2):
            own_copy(a, h).start()

    depth = w_hbm.shape[0] // parts

    def w_copy(i):
        return pltpu.make_async_copy(
            w_hbm.at[i * depth:(i + 1) * depth, :], w_ref.at[i * depth:(i + 1) * depth, :], w_sem.at[i]
        )

    routes = routes_ref[...].astype(jnp.float32).T.astype(jnp.int32)
    gates = gates_ref[...].T
    blocks = mask_ref.shape[0]
    usable_blocks = mask_ref[...].astype(jnp.float32).T
    for b in range(blocks):
        mask_scr[:, b * BLK:(b + 1) * BLK] = jnp.broadcast_to(usable_blocks[:, b:b + 1], (blocks, BLK))
    for k in range(topk):
        qf[k] = queries_ref[:, k * HD:(k + 1) * HD].astype(jnp.float32)
        rb[k] = jnp.broadcast_to(routes[:, k:k + 1], (tok, HD))
        gb[k] = jnp.broadcast_to(gates[:, k:k + 1], (tok, HD))

    pl.semaphore_wait(
        barrier, n + (chip > 0).astype(jnp.int32) + (chip < chips - 1).astype(jnp.int32)
    )

    def x_copy(a, h, k):
        block = kv.at[a, h, own_rows(k * 2 + core), :]
        return pltpu.make_async_remote_copy(
            src_ref=block, dst_ref=block, send_sem=x_send.at[a, h, k], recv_sem=x_recv.at[a, h, k],
            device_id=at(me, cx + 2), device_id_type=MESH,
        )

    def x_first(a, h):
        return pltpu.make_async_remote_copy(
            src_ref=sources[a].at[:, head_cols(h)], dst_ref=kv.at[a, h, own_rows(cx), :],
            send_sem=x_send.at[a, h, chips - 1], recv_sem=x_recv.at[a, h, chip],
            device_id=at(me, cx + 2), device_id_type=MESH,
        )

    def s_copy(a, h, k):
        block = kv.at[a, h, own_rows(k * 2 + core), :]
        return pltpu.make_async_remote_copy(
            src_ref=block, dst_ref=block, send_sem=s_send.at[a, h, k], recv_sem=s_recv.at[a, h, k],
            device_id=at(me, sibling), device_id_type=MESH,
        )

    def s_wait(a, h, k):
        block = kv.at[a, h, own_rows(k * 2 + (1 - core)), :]
        pltpu.make_async_remote_copy(
            src_ref=block, dst_ref=block, send_sem=s_send.at[a, h, k], recv_sem=s_recv.at[a, h, k],
            device_id=at(me, sibling), device_id_type=MESH,
        ).wait_recv()

    @pl.when(chip < chips - 1)
    def _():
        @pl.loop(0, per_dev)
        def _(h):
            for a in range(2):
                x_first(a, h).start()

    for i in range(parts):
        w_copy(i).start()

    def slot_of(source, dest):
        return lax.rem(source + dest, 2) * m + source // 2

    def q_copy(i):
        dest = lax.rem(me + i, n)
        return pltpu.make_async_remote_copy(
            src_ref=qsend.at[i], dst_ref=qall.at[slot_of(me, dest)], send_sem=q_send.at[i], recv_sem=q_recv.at[i],
            device_id=at(dest, cx), device_id_type=MESH,
        )

    def g_copy(i):
        dest = lax.rem(me + i, n)
        return pltpu.make_async_remote_copy(
            src_ref=gsend.at[i], dst_ref=gall.at[slot_of(me, dest)], send_sem=g_send.at[i], recv_sem=g_recv.at[i],
            device_id=at(dest, cx), device_id_type=MESH,
        )

    def spread(i):
        first = lax.rem(me + i, n) * per_dev
        acc = [jnp.zeros((tok, HD), jnp.float32) for _ in range(per_dev)]
        gate = jnp.zeros((tok, HD), jnp.float32)
        lane = lax.broadcasted_iota(jnp.int32, (tok, HD), 1) + first
        for k in range(topk):
            head, q = rb[k], qf[k]
            for j in range(per_dev):
                acc[j] = jnp.where(head == first + j, q, acc[j])
            gate = jnp.where(head == lane, gb[k], gate)
        return jnp.concatenate([a.astype(jnp.bfloat16) for a in acc], axis=1), gate

    @pl.loop(1, n)
    def _(i):
        q, gate = spread(i)
        qsend[i] = q
        gsend[i] = gate
        q_copy(i).start()
        g_copy(i).start()

    q, gate = spread(0)
    qall[z] = q
    gall[z] = gate

    @pl.loop(0, per_dev)
    def _(h):
        for a in range(2):
            own_copy(a, h).wait()
            s_copy(a, h, chip).start()

    @pl.loop(0, n)
    def _(slot):
        source = lax.rem(slot, m) * 2 + jnp.where(slot < m, y, 1 - y)
        base = cx * ctx_tok + source * tok
        qblock = base // BLK
        row = mask_scr[pl.ds(qblock, 1), :]
        kpos = lax.broadcasted_iota(jnp.int32, (tok, seq), 1)
        qpos = lax.broadcasted_iota(jnp.int32, (tok, seq), 0) + base
        kstart = qblock * BLK
        usable = ((row > 0.5) & (kpos < kstart)) | (kpos >= kstart)
        bias[pl.ds(pl.multiple_of(slot * tok, tok), tok), :] = jnp.where(
            usable & (kpos <= qpos), 0.0, -1e30
        ).astype(bias.dtype)

    @pl.loop(chip * 2 + 2, ctxs)
    def _(c):
        @pl.loop(0, per_dev)
        def _(h):
            for a in range(2):
                kv[a, h, own_rows(c), :] = jnp.zeros((ctx_tok, HD), jnp.bfloat16)

    @pl.loop(1, n)
    def _(i):
        source = lax.rem(me + n - i, n)
        slot = slot_of(source, me)
        pltpu.make_async_remote_copy(
            src_ref=qsend.at[i], dst_ref=qall.at[slot], send_sem=q_send.at[i], recv_sem=q_recv.at[i],
            device_id=at(source, cx), device_id_type=MESH,
        ).wait_recv()
        pltpu.make_async_remote_copy(
            src_ref=gsend.at[i], dst_ref=gall.at[slot], send_sem=g_send.at[i], recv_sem=g_recv.at[i],
            device_id=at(source, cx), device_id_type=MESH,
        ).wait_recv()

    scale = math.log2(math.e) / math.sqrt(HD)
    tile = max(tok, min(rows, (256 * 1024 // seq) // tok * tok))

    def forward(h):
        @pl.loop(0, chip)
        def _(k):
            for a in range(2):
                x_copy(a, h, k).wait_recv()
                s_copy(a, h, k).start()

            @pl.when(chip < chips - 1)
            def _():
                for a in range(2):
                    x_copy(a, h, k).start()

    def attend(h):
        @pl.loop(0, chip + 1)
        def _(k):
            for a in range(2):
                s_wait(a, h, k)

        def one(t):
            group = pl.ds(t * (tile // tok), tile // tok)
            here = pl.ds(pl.multiple_of(t * tile, tile), tile)
            q = qall[group, :, head_cols(h)].reshape(tile, HD)
            s = lax.dot_general(q, kv[0, h], (((1,), (1,)), ((), ())), preferred_element_type=jnp.float32)
            s = s * scale + bias[here, :].astype(jnp.float32)
            p = jnp.exp2(s - jnp.max(s, axis=1, keepdims=True))
            total = jnp.sum(p, axis=1, keepdims=True)
            o = jnp.dot(p.astype(jnp.bfloat16), kv[1, h], preferred_element_type=jnp.float32)
            lane = lax.broadcasted_iota(jnp.int32, (tile, HD), 1)
            gate = gall[group].reshape(tile, HD)
            g = jnp.sum(jnp.where(lane == h, gate, 0.0), axis=1, keepdims=True)
            weighted[here, head_cols(h)] = (o * (g / total)).astype(jnp.bfloat16)

        if rows == tile:
            one(0)
        else:
            pl.loop(0, rows // tile)(one)

    @pl.loop(0, per_dev + 1)
    def _(h):
        @pl.when(h < per_dev)
        def _():
            forward(h)

        @pl.when(h >= 1)
        def _():
            attend(h - 1)

    for i in range(parts):
        w_copy(i).wait()

    half = m * tok

    def y_copy(c):
        return pltpu.make_async_remote_copy(
            src_ref=ysend.at[c], dst_ref=yrecv.at[c], send_sem=y_send.at[c], recv_sem=y_recv.at[c],
            device_id=at(z * 2 + 1 - y, cx), device_id_type=MESH,
        )

    def up_copy(c, d):
        return pltpu.make_async_remote_copy(
            src_ref=psum.at[c, d], dst_ref=zrecv.at[c, d + 1], send_sem=up_send.at[c, d], recv_sem=up_recv.at[c, d],
            device_id=at(me + 2, cx), device_id_type=MESH,
        )

    def dn_copy(c, d):
        return pltpu.make_async_remote_copy(
            src_ref=psum.at[c, d], dst_ref=zrecv.at[c, d], send_sem=dn_send.at[c, d], recv_sem=dn_recv.at[c, d],
            device_id=at(me - 2, cx), device_id_type=MESH,
        )

    def add(c, d, got):
        psum[c, d] = (psum[c, d].astype(jnp.float32) + zrecv[c, got].astype(jnp.float32)).astype(jnp.bfloat16)

    @pl.loop(0, count + m - 1 + LAG)
    def _(i):
        @pl.when(i < count)
        def _():
            part = jnp.dot(
                weighted[...], w_ref[:, pl.ds(pl.multiple_of(i * cw, cw), cw)],
                preferred_element_type=jnp.float32,
            ).astype(jnp.bfloat16)
            ysend[i] = part[half:]
            psum[i] = part[:half].reshape(m, tok, cw)
            y_copy(i).start()

        @pl.when((i >= LAG) & (i < count + LAG))
        def _():
            c = i - LAG
            y_copy(c).wait_recv()
            psum[c] = (
                psum[c].astype(jnp.float32) + yrecv[c].astype(jnp.float32).reshape(m, tok, cw)
            ).astype(jnp.bfloat16)

        cu = i - LAG - z
        cd = i - LAG - (m - 1 - z)

        @pl.when((cu >= 0) & (cu < count))
        def _():
            for d in range(m - 1, -1, -1):
                @pl.when((z > 0) & (z <= d))
                def _():
                    up_copy(cu, d).wait_recv()

                @pl.when(z < d)
                def _():
                    @pl.when(z > 0)
                    def _():
                        add(cu, d, d + 1)
                    up_copy(cu, d).start()

        @pl.when((cd >= 0) & (cd < count))
        def _():
            for d in range(m):
                @pl.when((z < m - 1) & (z >= d))
                def _():
                    dn_copy(cd, d).wait_recv()

                @pl.when(z > d)
                def _():
                    @pl.when(z < m - 1)
                    def _():
                        add(cd, d, d)
                    dn_copy(cd, d).start()

        @pl.when(i >= m - 1 + LAG)
        def _():
            c = i - (m - 1 + LAG)
            cols = pl.ds(pl.multiple_of(c * cw, cw), cw)
            for d in range(m):
                @pl.when(z == d)
                def _():
                    total = psum[c, d].astype(jnp.float32)
                    if d > 0:
                        total = total + zrecv[c, d + 1].astype(jnp.float32)
                    if d < m - 1:
                        total = total + zrecv[c, d].astype(jnp.float32)
                    out_ref[:, cols] = total.astype(jnp.bfloat16)

    @pl.loop(0, count)
    def _(c):
        y_copy(c).wait_send()
        for d in range(m):
            @pl.when(z < d)
            def _():
                up_copy(c, d).wait_send()

            @pl.when(z > d)
            def _():
                dn_copy(c, d).wait_send()

    @pl.loop(1, n)
    def _(i):
        q_copy(i).wait_send()
        g_copy(i).wait_send()

    @pl.loop(0, per_dev)
    def _(h):
        for a in range(2):
            @pl.loop(0, chip + 1)
            def _(k):
                s_copy(a, h, k).wait_send()

            @pl.when(chip < chips - 1)
            def _():
                x_first(a, h).wait_send()

                @pl.loop(0, chip)
                def _(k):
                    x_copy(a, h, k).wait_send()


def local(n, ctxs, queries, keys, values, routes, gates, block_mask, w_out):
    tok, topk = routes.shape
    ctx_tok, held = keys.shape
    per_dev = held // HD
    seq = ctx_tok * ctxs
    rows = tok * n
    depth, width = w_out.shape
    m = n // 2
    chips = ctxs // 2
    blocks = block_mask.shape[0]
    count = width // CHUNK
    bf, f32, dma = jnp.bfloat16, jnp.float32, pltpu.SemaphoreType.DMA
    vmem = pl.BlockSpec(memory_space=pltpu.VMEM)
    hbm = pl.BlockSpec(memory_space=pl.ANY)
    return pl.pallas_call(
        functools.partial(kernel, n, ctxs),
        out_shape=jax.ShapeDtypeStruct((tok, width), bf),
        in_specs=[vmem, hbm, hbm, vmem, vmem, vmem, hbm],
        out_specs=vmem,
        scratch_shapes=[
            pltpu.VMEM((blocks, seq), f32),
            pltpu.VMEM((topk, tok, HD), f32),
            pltpu.VMEM((topk, tok, HD), jnp.int32),
            pltpu.VMEM((topk, tok, HD), f32),
            pltpu.VMEM((n, tok, held), bf),
            pltpu.VMEM((n, tok, HD), f32),
            pltpu.VMEM((n, tok, held), bf),
            pltpu.VMEM((n, tok, HD), f32),
            pltpu.VMEM((2, per_dev, seq, HD), bf),
            pltpu.VMEM((rows, seq), bf),
            pltpu.VMEM((rows, held), bf),
            pltpu.VMEM((depth, width), bf),
            pltpu.VMEM((count, m * tok, CHUNK), bf),
            pltpu.VMEM((count, m * tok, CHUNK), bf),
            pltpu.VMEM((count, m, tok, CHUNK), bf),
            pltpu.VMEM((count, m + 1, tok, CHUNK), bf),
            dma((8,)),
            dma((2, per_dev)),
            dma((2, per_dev, chips)),
            dma((2, per_dev, chips)),
            dma((2, per_dev, chips)),
            dma((2, per_dev, chips)),
            dma((n,)),
            dma((n,)),
            dma((n,)),
            dma((n,)),
            dma((count,)),
            dma((count,)),
            dma((count, m)),
            dma((count, m)),
            dma((count, m)),
            dma((count, m)),
        ],
        compiler_params=pltpu.CompilerParams(
            collective_id=0, has_side_effects=True, vmem_limit_bytes=63 * 1024 * 1024
        ),
    )(queries, keys, values, routes.T, gates.T, block_mask.T, w_out)


def solution(mesh):
    placed = (
        P(("ctx", "head"), None),
        P("ctx", "head"),
        P("ctx", "head"),
        P(("ctx", "head"), None),
        P(("ctx", "head"), None),
        P(),
        P("head", None),
    )
    return jax.shard_map(
        functools.partial(local, mesh.shape["head"], mesh.shape["ctx"]),
        mesh=mesh, in_specs=placed, out_specs=P(("ctx", "head"), None), check_vma=False,
    )
```

```python
import functools
import math

import jax
import jax.numpy as jnp
from jax import lax
from jax.experimental import pallas as pl
from jax.experimental.pallas import tpu as pltpu
from jax.sharding import PartitionSpec as P

HD = 128
BLK = 128
CHUNK = 1024
LAG = 3
MESH = pl.DeviceIdType.MESH


def kernel(
    n, ctxs,
    queries_ref, keys_ref, values_ref, routes_ref, gates_ref, mask_ref, w_hbm,
    out_ref,
    mask_scr, qf, rb, gb, qsend, gsend, qall, gall, kv, bias, weighted, w_ref,
    ysend, yrecv, psum, zrecv,
    w_sem, own_sem, x_send, x_recv, s_send, s_recv, q_send, q_recv, g_send, g_recv,
    y_send, y_recv, up_send, up_recv, dn_send, dn_recv,
):
    me = lax.axis_index("head")
    cx = lax.axis_index("ctx")
    y, z, m = lax.rem(me, 2), me // 2, n // 2
    core, chip, chips = lax.rem(cx, 2), cx // 2, ctxs // 2
    topk, tok = routes_ref.shape
    ctx_tok = keys_ref.shape[0]
    per_dev = keys_ref.shape[1] // HD
    rows = tok * n
    seq = ctx_tok * ctxs
    width = w_hbm.shape[1]
    cw = ysend.shape[2]
    count = width // cw
    parts = w_sem.shape[0]
    sources = (keys_ref, values_ref)

    def at(head, ctx):
        return (head, ctx)

    sibling = chip * 2 + (1 - core)

    barrier = pltpu.get_barrier_semaphore()
    for i in range(1, n):
        pl.semaphore_signal(barrier, inc=1, device_id=at(lax.rem(me + i, n), cx), device_id_type=MESH)
    pl.semaphore_signal(barrier, inc=1, device_id=at(me, sibling), device_id_type=MESH)

    @pl.when(chip > 0)
    def _():
        pl.semaphore_signal(barrier, inc=1, device_id=at(me, cx - 2), device_id_type=MESH)

    @pl.when(chip < chips - 1)
    def _():
        pl.semaphore_signal(barrier, inc=1, device_id=at(me, cx + 2), device_id_type=MESH)

    def own_rows(c):
        return pl.ds(pl.multiple_of(c * ctx_tok, ctx_tok), ctx_tok)

    def head_cols(h):
        return pl.ds(pl.multiple_of(h * HD, HD), HD)

    def own_copy(a, h):
        return pltpu.make_async_copy(
            sources[a].at[:, head_cols(h)], kv.at[a, h, own_rows(cx), :], own_sem.at[a, h]
        )

    @pl.loop(0, per_dev)
    def _(h):
        for a in range(2):
            own_copy(a, h).start()

    depth = w_hbm.shape[0] // parts

    def w_copy(i):
        return pltpu.make_async_copy(
            w_hbm.at[i * depth:(i + 1) * depth, :], w_ref.at[i * depth:(i + 1) * depth, :], w_sem.at[i]
        )

    routes = routes_ref[...].astype(jnp.float32).T.astype(jnp.int32)
    gates = gates_ref[...].T
    blocks = mask_ref.shape[0]
    usable_blocks = mask_ref[...].astype(jnp.float32).T
    for b in range(blocks):
        mask_scr[:, b * BLK:(b + 1) * BLK] = jnp.broadcast_to(usable_blocks[:, b:b + 1], (blocks, BLK))
    for k in range(topk):
        qf[k] = queries_ref[:, k * HD:(k + 1) * HD].astype(jnp.float32)
        rb[k] = jnp.broadcast_to(routes[:, k:k + 1], (tok, HD))
        gb[k] = jnp.broadcast_to(gates[:, k:k + 1], (tok, HD))

    pl.semaphore_wait(
        barrier, n + (chip > 0).astype(jnp.int32) + (chip < chips - 1).astype(jnp.int32)
    )

    def x_copy(a, h, k):
        block = kv.at[a, h, own_rows(k * 2 + core), :]
        return pltpu.make_async_remote_copy(
            src_ref=block, dst_ref=block, send_sem=x_send.at[a, h, k], recv_sem=x_recv.at[a, h, k],
            device_id=at(me, cx + 2), device_id_type=MESH,
        )

    def x_first(a, h):
        return pltpu.make_async_remote_copy(
            src_ref=kv.at[a, h, own_rows(cx), :], dst_ref=kv.at[a, h, own_rows(cx), :],
            send_sem=x_send.at[a, h, chips - 1], recv_sem=x_recv.at[a, h, chip],
            device_id=at(me, cx + 2), device_id_type=MESH,
        )

    def s_copy(a, h, k):
        block = kv.at[a, h, own_rows(k * 2 + core), :]
        return pltpu.make_async_remote_copy(
            src_ref=block, dst_ref=block, send_sem=s_send.at[a, h, k], recv_sem=s_recv.at[a, h, k],
            device_id=at(me, sibling), device_id_type=MESH,
        )

    def s_wait(a, h, k):
        block = kv.at[a, h, own_rows(k * 2 + (1 - core)), :]
        pltpu.make_async_remote_copy(
            src_ref=block, dst_ref=block, send_sem=s_send.at[a, h, k], recv_sem=s_recv.at[a, h, k],
            device_id=at(me, sibling), device_id_type=MESH,
        ).wait_recv()

    @pl.loop(0, per_dev)
    def _(h):
        for a in range(2):
            own_copy(a, h).wait()

        @pl.when(chip < chips - 1)
        def _():
            for a in range(2):
                x_first(a, h).start()

    @pl.loop(0, per_dev)
    def _(h):
        for a in range(2):
            s_copy(a, h, chip).start()

    for i in range(parts):
        w_copy(i).start()

    def slot_of(source, dest):
        return lax.rem(source + dest, 2) * m + source // 2

    def q_copy(i):
        dest = lax.rem(me + i, n)
        return pltpu.make_async_remote_copy(
            src_ref=qsend.at[i], dst_ref=qall.at[slot_of(me, dest)], send_sem=q_send.at[i], recv_sem=q_recv.at[i],
            device_id=at(dest, cx), device_id_type=MESH,
        )

    def g_copy(i):
        dest = lax.rem(me + i, n)
        return pltpu.make_async_remote_copy(
            src_ref=gsend.at[i], dst_ref=gall.at[slot_of(me, dest)], send_sem=g_send.at[i], recv_sem=g_recv.at[i],
            device_id=at(dest, cx), device_id_type=MESH,
        )

    def spread(i):
        first = lax.rem(me + i, n) * per_dev
        acc = [jnp.zeros((tok, HD), jnp.float32) for _ in range(per_dev)]
        gate = jnp.zeros((tok, HD), jnp.float32)
        lane = lax.broadcasted_iota(jnp.int32, (tok, HD), 1) + first
        for k in range(topk):
            head, q = rb[k], qf[k]
            for j in range(per_dev):
                acc[j] = jnp.where(head == first + j, q, acc[j])
            gate = jnp.where(head == lane, gb[k], gate)
        return jnp.concatenate([a.astype(jnp.bfloat16) for a in acc], axis=1), gate

    @pl.loop(1, n)
    def _(i):
        q, gate = spread(i)
        qsend[i] = q
        gsend[i] = gate
        q_copy(i).start()
        g_copy(i).start()

    q, gate = spread(0)
    qall[z] = q
    gall[z] = gate

    @pl.loop(0, n)
    def _(slot):
        source = lax.rem(slot, m) * 2 + jnp.where(slot < m, y, 1 - y)
        base = cx * ctx_tok + source * tok
        qblock = base // BLK
        row = mask_scr[pl.ds(qblock, 1), :]
        kpos = lax.broadcasted_iota(jnp.int32, (tok, seq), 1)
        qpos = lax.broadcasted_iota(jnp.int32, (tok, seq), 0) + base
        kstart = qblock * BLK
        usable = ((row > 0.5) & (kpos < kstart)) | (kpos >= kstart)
        bias[pl.ds(pl.multiple_of(slot * tok, tok), tok), :] = jnp.where(
            usable & (kpos <= qpos), 0.0, -1e30
        ).astype(bias.dtype)

    @pl.loop(chip * 2 + 2, ctxs)
    def _(c):
        @pl.loop(0, per_dev)
        def _(h):
            for a in range(2):
                kv[a, h, own_rows(c), :] = jnp.zeros((ctx_tok, HD), jnp.bfloat16)

    @pl.loop(1, n)
    def _(i):
        source = lax.rem(me + n - i, n)
        slot = slot_of(source, me)
        pltpu.make_async_remote_copy(
            src_ref=qsend.at[i], dst_ref=qall.at[slot], send_sem=q_send.at[i], recv_sem=q_recv.at[i],
            device_id=at(source, cx), device_id_type=MESH,
        ).wait_recv()
        pltpu.make_async_remote_copy(
            src_ref=gsend.at[i], dst_ref=gall.at[slot], send_sem=g_send.at[i], recv_sem=g_recv.at[i],
            device_id=at(source, cx), device_id_type=MESH,
        ).wait_recv()

    scale = math.log2(math.e) / math.sqrt(HD)
    tile = max(tok, min(rows, (256 * 1024 // seq) // tok * tok))

    def forward(h):
        @pl.loop(0, chip)
        def _(k):
            for a in range(2):
                x_copy(a, h, k).wait_recv()
                s_copy(a, h, k).start()

            @pl.when(chip < chips - 1)
            def _():
                for a in range(2):
                    x_copy(a, h, k).start()

    def attend(h):
        @pl.loop(0, chip + 1)
        def _(k):
            for a in range(2):
                s_wait(a, h, k)

        def one(t):
            group = pl.ds(t * (tile // tok), tile // tok)
            here = pl.ds(pl.multiple_of(t * tile, tile), tile)
            q = qall[group, :, head_cols(h)].reshape(tile, HD)
            s = lax.dot_general(q, kv[0, h], (((1,), (1,)), ((), ())), preferred_element_type=jnp.float32)
            s = s * scale + bias[here, :].astype(jnp.float32)
            p = jnp.exp2(s - jnp.max(s, axis=1, keepdims=True))
            total = jnp.sum(p, axis=1, keepdims=True)
            o = jnp.dot(p.astype(jnp.bfloat16), kv[1, h], preferred_element_type=jnp.float32)
            lane = lax.broadcasted_iota(jnp.int32, (tile, HD), 1)
            gate = gall[group].reshape(tile, HD)
            g = jnp.sum(jnp.where(lane == h, gate, 0.0), axis=1, keepdims=True)
            weighted[here, head_cols(h)] = (o * (g / total)).astype(jnp.bfloat16)

        if rows == tile:
            one(0)
        else:
            pl.loop(0, rows // tile)(one)

    @pl.loop(0, per_dev + 1)
    def _(h):
        @pl.when(h < per_dev)
        def _():
            forward(h)

        @pl.when(h >= 1)
        def _():
            attend(h - 1)

    for i in range(parts):
        w_copy(i).wait()

    half = m * tok

    def y_copy(c):
        return pltpu.make_async_remote_copy(
            src_ref=ysend.at[c], dst_ref=yrecv.at[c], send_sem=y_send.at[c], recv_sem=y_recv.at[c],
            device_id=at(z * 2 + 1 - y, cx), device_id_type=MESH,
        )

    def up_copy(c, d):
        return pltpu.make_async_remote_copy(
            src_ref=psum.at[c, d], dst_ref=zrecv.at[c, d + 1], send_sem=up_send.at[c, d], recv_sem=up_recv.at[c, d],
            device_id=at(me + 2, cx), device_id_type=MESH,
        )

    def dn_copy(c, d):
        return pltpu.make_async_remote_copy(
            src_ref=psum.at[c, d], dst_ref=zrecv.at[c, d], send_sem=dn_send.at[c, d], recv_sem=dn_recv.at[c, d],
            device_id=at(me - 2, cx), device_id_type=MESH,
        )

    def add(c, d, got):
        psum[c, d] = (psum[c, d].astype(jnp.float32) + zrecv[c, got].astype(jnp.float32)).astype(jnp.bfloat16)

    @pl.loop(0, count + m - 1 + LAG)
    def _(i):
        @pl.when(i < count)
        def _():
            part = jnp.dot(
                weighted[...], w_ref[:, pl.ds(pl.multiple_of(i * cw, cw), cw)],
                preferred_element_type=jnp.float32,
            ).astype(jnp.bfloat16)
            ysend[i] = part[half:]
            psum[i] = part[:half].reshape(m, tok, cw)
            y_copy(i).start()

        @pl.when((i >= LAG) & (i < count + LAG))
        def _():
            c = i - LAG
            y_copy(c).wait_recv()
            psum[c] = (
                psum[c].astype(jnp.float32) + yrecv[c].astype(jnp.float32).reshape(m, tok, cw)
            ).astype(jnp.bfloat16)

        cu = i - LAG - z
        cd = i - LAG - (m - 1 - z)

        @pl.when((cu >= 0) & (cu < count))
        def _():
            for d in range(m - 1, -1, -1):
                @pl.when((z > 0) & (z <= d))
                def _():
                    up_copy(cu, d).wait_recv()

                @pl.when(z < d)
                def _():
                    @pl.when(z > 0)
                    def _():
                        add(cu, d, d + 1)
                    up_copy(cu, d).start()

        @pl.when((cd >= 0) & (cd < count))
        def _():
            for d in range(m):
                @pl.when((z < m - 1) & (z >= d))
                def _():
                    dn_copy(cd, d).wait_recv()

                @pl.when(z > d)
                def _():
                    @pl.when(z < m - 1)
                    def _():
                        add(cd, d, d)
                    dn_copy(cd, d).start()

        @pl.when(i >= m - 1 + LAG)
        def _():
            c = i - (m - 1 + LAG)
            cols = pl.ds(pl.multiple_of(c * cw, cw), cw)
            for d in range(m):
                @pl.when(z == d)
                def _():
                    total = psum[c, d].astype(jnp.float32)
                    if d > 0:
                        total = total + zrecv[c, d + 1].astype(jnp.float32)
                    if d < m - 1:
                        total = total + zrecv[c, d].astype(jnp.float32)
                    out_ref[:, cols] = total.astype(jnp.bfloat16)

    @pl.loop(0, count)
    def _(c):
        y_copy(c).wait_send()
        for d in range(m):
            @pl.when(z < d)
            def _():
                up_copy(c, d).wait_send()

            @pl.when(z > d)
            def _():
                dn_copy(c, d).wait_send()

    @pl.loop(1, n)
    def _(i):
        q_copy(i).wait_send()
        g_copy(i).wait_send()

    @pl.loop(0, per_dev)
    def _(h):
        for a in range(2):
            @pl.loop(0, chip + 1)
            def _(k):
                s_copy(a, h, k).wait_send()

            @pl.when(chip < chips - 1)
            def _():
                x_first(a, h).wait_send()

                @pl.loop(0, chip)
                def _(k):
                    x_copy(a, h, k).wait_send()


def local(n, ctxs, queries, keys, values, routes, gates, block_mask, w_out):
    tok, topk = routes.shape
    ctx_tok, held = keys.shape
    per_dev = held // HD
    seq = ctx_tok * ctxs
    rows = tok * n
    depth, width = w_out.shape
    m = n // 2
    chips = ctxs // 2
    blocks = block_mask.shape[0]
    count = width // CHUNK
    bf, f32, dma = jnp.bfloat16, jnp.float32, pltpu.SemaphoreType.DMA
    vmem = pl.BlockSpec(memory_space=pltpu.VMEM)
    hbm = pl.BlockSpec(memory_space=pl.ANY)
    return pl.pallas_call(
        functools.partial(kernel, n, ctxs),
        out_shape=jax.ShapeDtypeStruct((tok, width), bf),
        in_specs=[vmem, hbm, hbm, vmem, vmem, vmem, hbm],
        out_specs=vmem,
        scratch_shapes=[
            pltpu.VMEM((blocks, seq), f32),
            pltpu.VMEM((topk, tok, HD), f32),
            pltpu.VMEM((topk, tok, HD), jnp.int32),
            pltpu.VMEM((topk, tok, HD), f32),
            pltpu.VMEM((n, tok, held), bf),
            pltpu.VMEM((n, tok, HD), f32),
            pltpu.VMEM((n, tok, held), bf),
            pltpu.VMEM((n, tok, HD), f32),
            pltpu.VMEM((2, per_dev, seq, HD), bf),
            pltpu.VMEM((rows, seq), bf),
            pltpu.VMEM((rows, held), bf),
            pltpu.VMEM((depth, width), bf),
            pltpu.VMEM((count, m * tok, CHUNK), bf),
            pltpu.VMEM((count, m * tok, CHUNK), bf),
            pltpu.VMEM((count, m, tok, CHUNK), bf),
            pltpu.VMEM((count, m + 1, tok, CHUNK), bf),
            dma((8,)),
            dma((2, per_dev)),
            dma((2, per_dev, chips)),
            dma((2, per_dev, chips)),
            dma((2, per_dev, chips)),
            dma((2, per_dev, chips)),
            dma((n,)),
            dma((n,)),
            dma((n,)),
            dma((n,)),
            dma((count,)),
            dma((count,)),
            dma((count, m)),
            dma((count, m)),
            dma((count, m)),
            dma((count, m)),
        ],
        compiler_params=pltpu.CompilerParams(
            collective_id=0, has_side_effects=True, vmem_limit_bytes=63 * 1024 * 1024
        ),
    )(queries, keys, values, routes.T, gates.T, block_mask.T, w_out)


def solution(mesh):
    placed = (
        P(("ctx", "head"), None),
        P("ctx", "head"),
        P("ctx", "head"),
        P(("ctx", "head"), None),
        P(("ctx", "head"), None),
        P(),
        P("head", None),
    )
    return jax.shard_map(
        functools.partial(local, mesh.shape["head"], mesh.shape["ctx"]),
        mesh=mesh, in_specs=placed, out_specs=P(("ctx", "head"), None), check_vma=False,
    )
```
